32 devices in a mesh: seq: 8 (over y, x, core), heads: 4 (over z).
Axes of the slice: x: 2, y: 2, z: 4, core: 2. Of those that a mesh axis runs over, the one named last changes fastest.
Arguments:
- hidden_in: bfloat16 [2048, 8192], P('seq', 'heads'), may hold values from -6 to 6
- queries: bfloat16 [2048, 8192], P('seq', 'heads'), as said below
- image_kv: bfloat16 [8, 2, 6528, 1024], P('seq', None, None, 'heads'), as said below
- out_weight: bfloat16 [8192, 8192], P('seq', 'heads'), may hold values from -0.0625 to 0.0625
- gate: float32 [1], replicated, may hold values from 0.4 to 1.2
- tile_counts: int32 [8], replicated, may hold values from 1 to 4, as said below
- owners: int32 [128], replicated, may hold values from 0 to 7, as said below
- starts: int32 [128], replicated, may hold values from 0 to 3, as said below
- norm_gain: float32 [8192], P('heads'), may hold values from 0.1 to 1.9
- norm_grad: bfloat16 [2048, 8192], P('seq', 'heads'), may hold values from -6 to 6
- stream_grad: bfloat16 [2048, 8192], P('seq', 'heads'), may hold values from -6 to 6
Outputs:
- hidden_out: bfloat16 [2048, 8192], P('seq', 'heads')
- stream_in_grad: float32 [2048, 8192], P('seq', 'heads')
The draws below stay inside these ranges and needn't reach their ends.
Inputs may be any that keep to these rules, and one draw needn't show every extreme that they name: `tile_counts`: tiles of each image; some image has 4 tiles in every draw. `owners`: the image (named by the seq index that owns it) that a block of 16 text rows attends to; of the 16 blocks of one seq index at most 2 name the same image, and in every draw some image is named by exactly 2 blocks of every seq index. `starts`: the first tile a block sees, below the tile count of the block's image; in every draw some block starts at tile 0 and some at tile 4 - 1. `image_kv`: keys and values are real-valued. real-valued queries.
All inputs are finite; a program needn't handle non-finite values.
Results may differ from the reference program's by a relative error of at most 0.007.
Values may be sent and summed in bfloat16 or wider, within the bound.
A program may use at most 128 MiB of HBM per device.

```python
import math
import jax
import jax.numpy as jnp
from jax import lax

D = 8192
HEADS = 64
KV_HEADS = 8
HEAD_DIM = 128
TILE_TOK = 1601
TILES_MAX = 4
TOK_DEV = 256
BLOCKS_DEV = 16
CAP = 2
BLK = 16
KEY_CAP = 6528
TOKENS = 2048
NBLK = 128
N_SEQ = 8


def layout(key):
    base = jax.random.fold_in(key, 7)
    keys = jax.random.split(base, 10)
    counts = jax.random.randint(keys[0], (N_SEQ,), 1, TILES_MAX + 1)
    hottest = jax.random.randint(keys[2], (), 0, N_SEQ)
    fullest = (hottest + 1 + jax.random.randint(keys[9], (), 0, N_SEQ - 1)) % N_SEQ
    counts = jnp.where(jnp.arange(N_SEQ) == fullest, TILES_MAX, counts)
    slots = jnp.arange(N_SEQ * CAP)
    ranking = jax.random.randint(keys[3], (N_SEQ, N_SEQ * CAP), 0, 1 << 20) * (N_SEQ * CAP) + slots[None, :]
    ranking = jnp.where((slots // CAP == fullest)[None, :], -1 - slots[None, :], ranking)
    ranking = jnp.where((slots // CAP == hottest)[None, :], -(1 << 22) - slots[None, :], ranking)
    ordered = jnp.argsort(ranking, axis=1)[:, :BLOCKS_DEV]
    chosen = ordered // CAP
    mixing = jax.vmap(lambda sub: jax.random.permutation(sub, BLOCKS_DEV))(jax.random.split(keys[4], N_SEQ))
    owners = jnp.take_along_axis(chosen, mixing, axis=1).reshape(-1)
    span = counts[owners]
    starts = jax.random.randint(keys[5], (N_SEQ * BLOCKS_DEV,), 0, 1 << 20) % span
    total_blocks = N_SEQ * BLOCKS_DEV
    marked = (owners == fullest).astype(jnp.int32)
    first_full = jnp.argmax(marked)
    last_full = total_blocks - 1 - jnp.argmax(marked[::-1])
    places = jnp.arange(total_blocks)
    starts = jnp.where(places == first_full, TILES_MAX - 1, starts)
    starts = jnp.where(places == last_full, 0, starts)
    return (counts, owners, starts)


def draw_tile_counts(key, part):
    return layout(key)[0].astype(jnp.int32)


def draw_owners(key, part):
    return layout(key)[1].astype(jnp.int32)


def draw_starts(key, part):
    return layout(key)[2].astype(jnp.int32)


def draw_image_kv(key, part):
    body_key = jax.random.fold_in(key, 11)
    shape = (N_SEQ, 2, KEY_CAP, KV_HEADS * HEAD_DIM)
    factor = jnp.array([2.0, 4.0], jnp.float32).reshape(1, 2, 1, 1)
    values = jax.random.truncated_normal(body_key, -4.0, 4.0, shape, jnp.float32) * factor
    return values.astype(jnp.bfloat16)


def draw_queries(key, part):
    body_key = jax.random.fold_in(key, 13)
    shape = (N_SEQ * TOK_DEV, D)
    values = jax.random.truncated_normal(body_key, -4.0, 4.0, shape, jnp.float32)
    return values.astype(jnp.bfloat16)


def block_levels(own_key, shape, cuts, smallest, top_value):
    def one(position, parts):
        draws = jax.random.uniform(jax.random.fold_in(jax.random.fold_in(own_key, 6), position), (parts,), jnp.float32, smallest / len(cuts), top_value / len(cuts))
        return jnp.repeat(jnp.exp(draws), shape[position] // parts).reshape((-1,) + (1,) * (len(shape) - position - 1))

    factor_of = one(*cuts[0])
    for cut in cuts[1:]:
        factor_of = factor_of * one(*cut)
    return factor_of


def noise(key, shape, spread, limit, cuts=(), dtype=jnp.bfloat16):
    gain = block_levels(key, shape, cuts, -0.22, 0.18) if cuts else 1.0
    drawn = jax.random.normal(key, shape, jnp.float32) * spread * gain
    return jnp.minimum(jnp.maximum(drawn, -limit), limit).astype(dtype)


def setup_inputs(seed: int = 0) -> dict:
    key_list = jax.random.split(jax.random.key(seed), 12)
    return {
        "hidden_in": noise(key_list[0], (TOKENS, D), 1.0, 6.0, ((0, 8), (1, 4))),
        "queries": draw_queries(jax.random.fold_in(key_list[11], 71), 0),
        "image_kv": draw_image_kv(jax.random.fold_in(key_list[11], 71), 0),
        "out_weight": noise(key_list[3], (D, D), D ** -0.5, 0.0625, ((0, 8), (1, 4))),
        "gate": jnp.clip(jax.random.uniform(key_list[4], (1,), jnp.float32, 0.4, 1.2), 0.4, 1.2),
        "tile_counts": draw_tile_counts(jax.random.fold_in(key_list[11], 71), 0),
        "owners": draw_owners(jax.random.fold_in(key_list[11], 71), 0),
        "starts": draw_starts(jax.random.fold_in(key_list[11], 71), 0),
        "norm_gain": jnp.clip(1.0 + 0.18 * jax.random.normal(key_list[8], (D,), jnp.float32), 0.1, 1.9),
        "norm_grad": noise(key_list[9], (TOKENS, D), 1.0, 6.0, ((0, 8), (1, 4))),
        "stream_grad": noise(key_list[10], (TOKENS, D), 1.0, 6.0, ((0, 8), (1, 4))),
    }


EPS = 1e-05

def attend_block(block, image_kv, tile_counts):
    rows, image, first = block
    pair = lax.dynamic_index_in_dim(image_kv, image, 0, keepdims=False).astype(jnp.float32)
    keys = pair[0].reshape(KEY_CAP, KV_HEADS, HEAD_DIM)
    values = pair[1].reshape(KEY_CAP, KV_HEADS, HEAD_DIM)
    grouped = rows.astype(jnp.float32).reshape(BLK, KV_HEADS, HEADS // KV_HEADS, HEAD_DIM)
    scale = 1.0 / math.sqrt(HEAD_DIM)
    scores = jnp.einsum('rkgd,nkd->kgrn', grouped, keys) * scale
    spot = jnp.arange(KEY_CAP).astype(jnp.int32)
    last = lax.dynamic_index_in_dim(tile_counts, image, 0, keepdims=False) * TILE_TOK
    seen = jnp.logical_and(spot >= first * TILE_TOK, spot < last)
    scores = jnp.where(seen, scores, -jnp.inf)
    highest = lax.optimization_barrier(jnp.max(scores, axis=-1, keepdims=True))
    probs = jnp.exp(scores - highest)
    total = lax.optimization_barrier(jnp.sum(probs, axis=-1, keepdims=True))
    weights = lax.optimization_barrier(probs.astype(jnp.bfloat16)).astype(jnp.float32)
    mixed = jnp.einsum('kgrn,nkd->kgrd', weights, values) / total
    return jnp.transpose(mixed, (2, 0, 1, 3)).reshape(BLK, HEADS * HEAD_DIM).astype(jnp.bfloat16)

def reference(hidden_in, queries, image_kv, out_weight, gate, tile_counts, owners, starts, norm_gain, norm_grad, stream_grad):
    q_blocks = queries.reshape(NBLK, BLK, D)
    context = lax.map(lambda block: attend_block(block, image_kv, tile_counts), (q_blocks, owners, starts))
    context = context.reshape(TOKENS, D)
    branch = jnp.dot(context, out_weight, preferred_element_type=jnp.float32)
    hidden_out = (hidden_in.astype(jnp.float32) + jnp.tanh(gate[0]) * branch).astype(jnp.bfloat16)
    hidden = hidden_out.astype(jnp.float32)
    scaled = norm_gain.astype(jnp.float32)[None, :] * norm_grad.astype(jnp.float32)
    inverse = lax.rsqrt(lax.optimization_barrier(jnp.mean(hidden * hidden, axis=1, keepdims=True)) + EPS)
    project = lax.optimization_barrier(jnp.mean(hidden * scaled, axis=1, keepdims=True))
    stream_in_grad = stream_grad.astype(jnp.float32) + inverse * scaled - inverse ** 3 * project * hidden
    return (hidden_out, stream_in_grad)
```

```python
import math

import jax
import jax.numpy as jnp
from jax import lax
from jax.experimental import pallas as pl
from jax.experimental.pallas import tpu as pltpu
from jax.sharding import PartitionSpec as P

D = 8192
HEAD_DIM = 128
TILE_TOK = 1601
BLOCKS_DEV = 16
CAP = 2
BLK = 16


EPS = 1e-05


KEY_BLOCK = 1792
KEY_PART = 256
LANES = 128
GROUP_SLOTS = 4


def attend_body(order_ref, first_ref, tiles_ref, q_ref, k_ref, v_ref, o_ref, qs, vx, acc, top):
    step = pl.program_id(0)
    heads = q_ref.shape[1] // HEAD_DIM
    per_head = GROUP_SLOTS * BLK
    rows = heads * per_head
    factor = math.log2(math.e) / math.sqrt(HEAD_DIM)

    @pl.when(step == 0)
    def _():
        vx[:, :HEAD_DIM] = v_ref[0, 0]
        vx[:, HEAD_DIM:] = jnp.ones((vx.shape[0], HEAD_DIM), jnp.bfloat16)

    for slot in range(GROUP_SLOTS):
        place = order_ref[step * GROUP_SLOTS + slot]
        source = q_ref[pl.ds(pl.multiple_of(place * BLK, BLK), BLK), :]
        for head in range(heads):
            qs[pl.ds(head * per_head + slot * BLK, BLK), :] = source[
                :, head * HEAD_DIM : (head + 1) * HEAD_DIM
            ]
    acc[...] = jnp.zeros_like(acc)
    top[...] = jnp.full_like(top, -3e38)
    slot_of = lax.broadcasted_iota(jnp.int32, (rows, LANES), 0) % per_head // BLK
    first = jnp.zeros((rows, LANES), jnp.int32)
    lowest = first_ref[step * GROUP_SLOTS]
    for slot in range(GROUP_SLOTS):
        first = jnp.where(slot_of == slot, first_ref[step * GROUP_SLOTS + slot], first)

    @pl.loop(lowest, tiles_ref[0])
    def _(tile):
        base = pl.multiple_of(tile * TILE_TOK // LANES * LANES, LANES)
        low = tile * TILE_TOK - base
        high = low + TILE_TOK
        query = qs[...]
        parts = []
        best = None
        for part in range(KEY_BLOCK // KEY_PART):
            keys = k_ref[0, 0, pl.ds(base + part * KEY_PART, KEY_PART), :]
            scores = lax.dot_general(
                query, keys, (((1,), (1,)), ((), ())), preferred_element_type=jnp.float32
            )
            spot = lax.broadcasted_iota(jnp.int32, scores.shape, 1) + part * KEY_PART
            if part == 0:
                scores = jnp.where(spot >= low, scores, -jnp.inf)
            if (part + 1) * KEY_PART > TILE_TOK:
                scores = jnp.where(spot < high, scores, -jnp.inf)
            parts.append(scores)
            peak = jnp.maximum(scores[:, :LANES], scores[:, LANES:])
            best = peak if best is None else jnp.maximum(best, peak)
        before = top[...]
        seen = first <= tile
        highest = jnp.maximum(before, jnp.max(best, axis=1, keepdims=True))
        highest = jnp.where(seen, highest, before)
        top[...] = highest
        alpha = jnp.exp2((before - highest) * factor)
        shift = jnp.where(seen, highest * factor, jnp.inf)
        shift = jnp.concatenate([shift, shift], axis=1)
        mixed = None
        for part in range(KEY_BLOCK // KEY_PART):
            probs = jnp.exp2(parts[part] * factor - shift).astype(jnp.bfloat16)
            values = vx[pl.ds(base + part * KEY_PART, KEY_PART), :]
            term = jnp.dot(probs, values, preferred_element_type=jnp.float32)
            mixed = term if mixed is None else mixed + term
        acc[...] = acc[...] * jnp.concatenate([alpha, alpha], axis=1) + mixed

    result = (acc[:, :HEAD_DIM] / acc[:, HEAD_DIM:]).astype(jnp.bfloat16)
    for slot in range(GROUP_SLOTS):
        place = order_ref[step * GROUP_SLOTS + slot]
        for head in range(heads):
            start = head * per_head + slot * BLK
            o_ref[
                pl.ds(pl.multiple_of(place * BLK, BLK), BLK),
                head * HEAD_DIM : (head + 1) * HEAD_DIM,
            ] = result[start : start + BLK]


def attend(order, first, tiles, flat, image_kv, index, width, kv_head):
    rows = flat.shape[0]
    keys = image_kv.shape[2]
    stacked = width // HEAD_DIM * GROUP_SLOTS * BLK
    return pl.pallas_call(
        attend_body,
        grid_spec=pltpu.PrefetchScalarGridSpec(
            num_scalar_prefetch=3,
            grid=(rows // (GROUP_SLOTS * BLK),),
            in_specs=[
                pl.BlockSpec((rows, width), lambda g, *_: (0, index)),
                pl.BlockSpec((1, 1, keys, HEAD_DIM), lambda g, *_: (0, 0, 0, kv_head)),
                pl.BlockSpec((1, 1, keys, HEAD_DIM), lambda g, *_: (0, 1, 0, kv_head)),
            ],
            out_specs=pl.BlockSpec((rows, width), lambda g, *_: (0, 0)),
            scratch_shapes=[
                pltpu.VMEM((stacked, HEAD_DIM), jnp.bfloat16),
                pltpu.VMEM((keys, 2 * HEAD_DIM), jnp.bfloat16),
                pltpu.VMEM((stacked, 2 * HEAD_DIM), jnp.float32),
                pltpu.VMEM((stacked, LANES), jnp.float32),
            ],
        ),
        out_shape=jax.ShapeDtypeStruct((rows, width), jnp.bfloat16),
        compiler_params=pltpu.CompilerParams(vmem_limit_bytes=40 * 2**20),
        cost_estimate=pl.CostEstimate(
            flops=4 * rows * width * keys,
            bytes_accessed=4 * keys * HEAD_DIM + 4 * rows * width,
            transcendentals=rows * width // HEAD_DIM * keys,
        ),
    )(order, first, tiles, flat, image_kv, image_kv)


def local(
    hidden_in,
    queries,
    image_kv,
    out_weight,
    gate,
    tile_counts,
    owners,
    starts,
    norm_gain,
    norm_grad,
    stream_grad,
):
    seq_count = lax.axis_size("seq")
    here = lax.axis_index("seq")
    tok_rows, q_width = queries.shape
    q_heads = q_width // HEAD_DIM
    kv_width = image_kv.shape[3]
    group = q_heads // (kv_width // HEAD_DIM)
    slot_count = seq_count * CAP
    owner_table = owners.reshape(seq_count, BLOCKS_DEV)
    start_table = starts.reshape(seq_count, BLOCKS_DEV)
    my_owner = lax.dynamic_index_in_dim(owner_table, here, 0, keepdims=False)
    block_ids = jnp.arange(BLOCKS_DEV)
    same = my_owner[:, None] == my_owner[None, :]
    earlier = block_ids[None, :] < block_ids[:, None]
    my_rank = jnp.sum(jnp.logical_and(same, earlier).astype(jnp.int32), axis=1)
    my_slot = my_owner * CAP + my_rank
    placing = (my_slot[:, None] == jnp.arange(slot_count)[None, :]).astype(jnp.bfloat16)
    q_blocks = queries.reshape(BLOCKS_DEV, BLK, q_width)
    outgoing = jnp.einsum(
        "bs,brc->src", placing, q_blocks, preferred_element_type=jnp.float32
    ).astype(jnp.bfloat16)
    outgoing = outgoing.reshape(seq_count, CAP, BLK, q_width)
    arriving = owner_table == here
    arrive_rank = jnp.cumsum(arriving.astype(jnp.int32), axis=1) - 1
    slot_hit = jnp.logical_and(
        arriving[:, :, None], arrive_rank[:, :, None] == jnp.arange(CAP)[None, None, :]
    )
    slot_start = jnp.sum(jnp.where(slot_hit, start_table[:, :, None], 0), axis=1)
    tile_here = lax.dynamic_index_in_dim(tile_counts, here, 0, keepdims=False)
    received = lax.all_to_all(outgoing, "seq", split_axis=0, concat_axis=0, tiled=True)
    flat = received.reshape(-1, q_width)
    slot_first = slot_start.reshape(-1)
    order = jnp.argsort(slot_first).astype(jnp.int32)
    sorted_first = slot_first[order]
    row_width = out_weight.shape[0]
    width = group * HEAD_DIM // 2
    pieces = row_width // width
    gathered = []
    for index in range(q_width // width):
        mixed = attend(
            order, sorted_first, tile_here[None], flat, image_kv, index, width, index // 2
        )
        gathered.append(lax.all_gather(mixed, "heads", axis=0))
    stacked = jnp.stack(gathered).reshape(-1, pieces, len(gathered[0]), flat.shape[0], width)
    outgoing = jnp.transpose(stacked, (2, 0, 3, 1, 4)).reshape(seq_count, flat.shape[0], row_width)
    feature_rows = lax.all_to_all(outgoing, "seq", split_axis=0, concat_axis=0, tiled=True)
    feature_rows = feature_rows.reshape(seq_count, seq_count, CAP * BLK, row_width)
    feature_rows = jnp.swapaxes(feature_rows, 0, 1).reshape(-1, row_width)
    slots = lax.psum_scatter(
        jnp.dot(feature_rows, out_weight, preferred_element_type=jnp.float32).astype(jnp.bfloat16),
        "seq",
        scatter_dimension=0,
        tiled=True,
    )
    branch = jnp.einsum(
        "bs,src->brc",
        placing,
        slots.reshape(slot_count, BLK, -1),
        preferred_element_type=jnp.float32,
    ).reshape(tok_rows, -1)
    hidden_out = (hidden_in.astype(jnp.float32) + jnp.tanh(gate[0]) * branch).astype(jnp.bfloat16)
    hidden = hidden_out.astype(jnp.float32)
    scaled = norm_gain[None, :] * norm_grad.astype(jnp.float32)
    squares, product = lax.psum(
        (jnp.sum(hidden * hidden, axis=1), jnp.sum(hidden * scaled, axis=1)), "heads"
    )
    inverse = lax.rsqrt(squares / D + EPS)[:, None]
    project = (product / D)[:, None]
    stream_in_grad = (
        stream_grad.astype(jnp.float32) + inverse * scaled - inverse**3 * project * hidden
    )
    return (hidden_out, stream_in_grad)


def solution(mesh):
    placed = (
        P("seq", "heads"),
        P("seq", "heads"),
        P("seq", None, None, "heads"),
        P("seq", "heads"),
        P(),
        P(),
        P(),
        P(),
        P("heads"),
        P("seq", "heads"),
        P("seq", "heads"),
    )
    return jax.shard_map(
        local,
        mesh=mesh,
        in_specs=placed,
        out_specs=(P("seq", "heads"), P("seq", "heads")),
        check_vma=False,
    )
```

```python
import functools
import math

import jax
import jax.numpy as jnp
from jax import lax
from jax.experimental import pallas as pl
from jax.experimental.pallas import tpu as pltpu
from jax.sharding import PartitionSpec as P

D = 8192
HEAD_DIM = 128
TILE_TOK = 1601
BLOCKS_DEV = 16
CAP = 2
BLK = 16


EPS = 1e-05


KEY_BLOCK = 1792
KEY_PART = 256
LANES = 128
GROUP_SLOTS = 4


def attend_body(order_ref, first_ref, tiles_ref, q_ref, k_ref, v_ref, o_ref, qs, vx, acc, top):
    step = pl.program_id(0)
    heads = q_ref.shape[1] // HEAD_DIM
    per_head = GROUP_SLOTS * BLK
    rows = heads * per_head
    factor = math.log2(math.e) / math.sqrt(HEAD_DIM)

    @pl.when(step == 0)
    def _():
        vx[:, :HEAD_DIM] = v_ref[0, 0]
        vx[:, HEAD_DIM:] = jnp.ones((vx.shape[0], HEAD_DIM), jnp.bfloat16)

    for slot in range(GROUP_SLOTS):
        place = order_ref[step * GROUP_SLOTS + slot]
        source = q_ref[pl.ds(pl.multiple_of(place * BLK, BLK), BLK), :]
        for head in range(heads):
            qs[pl.ds(head * per_head + slot * BLK, BLK), :] = source[
                :, head * HEAD_DIM : (head + 1) * HEAD_DIM
            ]
    acc[...] = jnp.zeros_like(acc)
    top[...] = jnp.full_like(top, -3e38)
    slot_of = lax.broadcasted_iota(jnp.int32, (rows, LANES), 0) % per_head // BLK
    first = jnp.zeros((rows, LANES), jnp.int32)
    lowest = first_ref[step * GROUP_SLOTS]
    for slot in range(GROUP_SLOTS):
        first = jnp.where(slot_of == slot, first_ref[step * GROUP_SLOTS + slot], first)

    @pl.loop(lowest, tiles_ref[0])
    def _(tile):
        base = pl.multiple_of(tile * TILE_TOK // LANES * LANES, LANES)
        low = tile * TILE_TOK - base
        high = low + TILE_TOK
        query = qs[...]
        parts = []
        best = None
        for part in range(KEY_BLOCK // KEY_PART):
            keys = k_ref[0, 0, pl.ds(base + part * KEY_PART, KEY_PART), :]
            scores = lax.dot_general(
                query, keys, (((1,), (1,)), ((), ())), preferred_element_type=jnp.float32
            )
            spot = lax.broadcasted_iota(jnp.int32, scores.shape, 1) + part * KEY_PART
            if part == 0:
                scores = jnp.where(spot >= low, scores, -jnp.inf)
            if (part + 1) * KEY_PART > TILE_TOK:
                scores = jnp.where(spot < high, scores, -jnp.inf)
            parts.append(scores)
            peak = jnp.maximum(scores[:, :LANES], scores[:, LANES:])
            best = peak if best is None else jnp.maximum(best, peak)
        before = top[...]
        seen = first <= tile
        highest = jnp.maximum(before, jnp.max(best, axis=1, keepdims=True))
        highest = jnp.where(seen, highest, before)
        top[...] = highest
        alpha = jnp.exp2((before - highest) * factor)
        shift = jnp.where(seen, highest * factor, jnp.inf)
        shift = jnp.concatenate([shift, shift], axis=1)
        mixed = None
        for part in range(KEY_BLOCK // KEY_PART):
            probs = jnp.exp2(parts[part] * factor - shift).astype(jnp.bfloat16)
            values = vx[pl.ds(base + part * KEY_PART, KEY_PART), :]
            term = jnp.dot(probs, values, preferred_element_type=jnp.float32)
            mixed = term if mixed is None else mixed + term
        acc[...] = acc[...] * jnp.concatenate([alpha, alpha], axis=1) + mixed

    result = (acc[:, :HEAD_DIM] / acc[:, HEAD_DIM:]).astype(jnp.bfloat16)
    for slot in range(GROUP_SLOTS):
        place = order_ref[step * GROUP_SLOTS + slot]
        for head in range(heads):
            start = head * per_head + slot * BLK
            o_ref[
                pl.ds(pl.multiple_of(place * BLK, BLK), BLK),
                head * HEAD_DIM : (head + 1) * HEAD_DIM,
            ] = result[start : start + BLK]


def attend(order, first, tiles, flat, image_kv, index, width, kv_head):
    rows = flat.shape[0]
    keys = image_kv.shape[2]
    stacked = width // HEAD_DIM * GROUP_SLOTS * BLK
    return pl.pallas_call(
        attend_body,
        grid_spec=pltpu.PrefetchScalarGridSpec(
            num_scalar_prefetch=3,
            grid=(rows // (GROUP_SLOTS * BLK),),
            in_specs=[
                pl.BlockSpec((rows, width), lambda g, *_: (0, index)),
                pl.BlockSpec((1, 1, keys, HEAD_DIM), lambda g, *_: (0, 0, 0, kv_head)),
                pl.BlockSpec((1, 1, keys, HEAD_DIM), lambda g, *_: (0, 1, 0, kv_head)),
            ],
            out_specs=pl.BlockSpec((rows, width), lambda g, *_: (0, 0)),
            scratch_shapes=[
                pltpu.VMEM((stacked, HEAD_DIM), jnp.bfloat16),
                pltpu.VMEM((keys, 2 * HEAD_DIM), jnp.bfloat16),
                pltpu.VMEM((stacked, 2 * HEAD_DIM), jnp.float32),
                pltpu.VMEM((stacked, LANES), jnp.float32),
            ],
        ),
        out_shape=jax.ShapeDtypeStruct((rows, width), jnp.bfloat16),
        compiler_params=pltpu.CompilerParams(vmem_limit_bytes=60 * 2**20),
        cost_estimate=pl.CostEstimate(
            flops=4 * rows * width * keys,
            bytes_accessed=4 * keys * HEAD_DIM + 4 * rows * width,
            transcendentals=rows * width // HEAD_DIM * keys,
        ),
    )(order, first, tiles, flat, image_kv, image_kv)


def project_body(seq_count, count, *refs):
    parts = refs[:count]
    w_ref, o_ref = refs[count : count + 2]
    (held, stage, paired, summed, landed, own) = refs[count + 2 : count + 8]
    (send_a, recv_a, send_p, recv_p, send_s, recv_s, local_sem) = refs[count + 8 :]
    me = lax.axis_index("seq")
    chips = seq_count // 2
    chip, core = me // 2, lax.rem(me, 2)
    sibling = chip * 2 + 1 - core
    splits = count
    rows, columns = own.shape
    tile = 512
    barrier = pltpu.get_barrier_semaphore()
    for step in range(1, seq_count):
        pl.semaphore_signal(
            barrier,
            inc=1,
            device_id={"seq": lax.rem(me + step, seq_count)},
            device_id_type=pl.DeviceIdType.MESH,
        )
    pl.semaphore_wait(barrier, seq_count - 1)

    def context_copy(part, step):
        target = lax.rem(me + step, seq_count)
        return pltpu.make_async_remote_copy(
            src_ref=parts[part].at[target // splits],
            dst_ref=held.at[:, me],
            send_sem=send_a.at[step],
            recv_sem=recv_a.at[step],
            device_id={"seq": target},
            device_id_type=pl.DeviceIdType.MESH,
        )

    for step in list(range(2, seq_count)) + [1]:
        for part in range(splits):
            @pl.when(lax.rem(me + step, splits) == part)
            def _():
                context_copy(part, step).start()

    for part in range(splits):
        @pl.when(lax.rem(me, splits) == part)
        def _():
            kept = pltpu.make_async_copy(
                parts[part].at[me // splits], held.at[:, me], local_sem
            )
            kept.start()
            kept.wait()

    for step in range(1, seq_count):
        source = lax.rem(me + seq_count - step, seq_count)
        pltpu.make_async_remote_copy(
            src_ref=parts[0].at[0],
            dst_ref=held.at[:, source],
            send_sem=send_a.at[step],
            recv_sem=recv_a.at[step],
            device_id={"seq": source},
            device_id_type=pl.DeviceIdType.MESH,
        ).wait_recv()

    def product(target, start):
        left = held[target].reshape(rows, held.shape[3])
        return jnp.dot(
            left, w_ref[:, pl.ds(start, tile)], preferred_element_type=jnp.float32
        )

    def target_chip(step):
        return lax.rem(chip + 1 + step, chips)

    def pair_copy(step):
        return pltpu.make_async_remote_copy(
            src_ref=stage.at[step],
            dst_ref=paired.at[step],
            send_sem=send_p.at[step],
            recv_sem=recv_p.at[step],
            device_id={"seq": sibling},
            device_id_type=pl.DeviceIdType.MESH,
        )

    def sum_copy(step):
        return pltpu.make_async_remote_copy(
            src_ref=summed.at[step],
            dst_ref=landed.at[step],
            send_sem=send_s.at[step],
            recv_sem=recv_s.at[step],
            device_id={"seq": target_chip(step) * 2 + core},
            device_id_type=pl.DeviceIdType.MESH,
        )

    def give(step):
        @pl.loop(0, columns // tile)
        def _(index):
            start = pl.multiple_of(index * tile, tile)
            stage[step, :, pl.ds(start, tile)] = product(
                target_chip(step) * 2 + 1 - core, start
            ).astype(jnp.bfloat16)

        pair_copy(step).start()

    give(0)
    for step in range(chips):
        if step + 1 < chips:
            give(step + 1)

        @pl.loop(0, columns // tile)
        def _(index):
            start = pl.multiple_of(index * tile, tile)
            own[:, pl.ds(start, tile)] = product(target_chip(step) * 2 + core, start)

        pair_copy(step).wait_recv()
        if step + 1 < chips:
            @pl.loop(0, columns // tile)
            def _(index):
                span = pl.ds(pl.multiple_of(index * tile, tile), tile)
                total = own[:, span] + paired[step, :, span].astype(jnp.float32)
                summed[step, :, span] = total.astype(jnp.bfloat16)

            sum_copy(step).start()

    for step in range(chips - 1):
        sum_copy(step).wait_recv()

    @pl.loop(0, columns // tile)
    def _(index):
        span = pl.ds(pl.multiple_of(index * tile, tile), tile)
        total = own[:, span] + paired[chips - 1, :, span].astype(jnp.float32)
        for step in range(chips - 1):
            total = total + landed[step, :, span].astype(jnp.float32)
        o_ref[:, span] = total.astype(jnp.bfloat16)

    for step in range(1, seq_count):
        context_copy(0, step).wait_send()
    for step in range(chips):
        pair_copy(step).wait_send()
    for step in range(chips - 1):
        sum_copy(step).wait_send()


def project_rows(parts, out_weight, seq_count):
    count = len(parts)
    depth, columns = out_weight.shape
    piece = parts[0].shape[2]
    rows = seq_count * piece
    chips = seq_count // 2
    return pl.pallas_call(
        functools.partial(project_body, seq_count, count),
        in_specs=[pl.BlockSpec(memory_space=pl.ANY)] * count
        + [pl.BlockSpec(memory_space=pltpu.VMEM)],
        out_specs=pl.BlockSpec(memory_space=pltpu.VMEM),
        out_shape=jax.ShapeDtypeStruct((rows, columns), jnp.bfloat16),
        scratch_shapes=[
            pltpu.VMEM((seq_count, seq_count, piece, depth), jnp.bfloat16),
            pltpu.VMEM((chips, rows, columns), jnp.bfloat16),
            pltpu.VMEM((chips, rows, columns), jnp.bfloat16),
            pltpu.VMEM((chips - 1, rows, columns), jnp.bfloat16),
            pltpu.VMEM((chips - 1, rows, columns), jnp.bfloat16),
            pltpu.VMEM((rows, columns), jnp.float32),
            pltpu.SemaphoreType.DMA((seq_count,)),
            pltpu.SemaphoreType.DMA((seq_count,)),
            pltpu.SemaphoreType.DMA((chips,)),
            pltpu.SemaphoreType.DMA((chips,)),
            pltpu.SemaphoreType.DMA((chips,)),
            pltpu.SemaphoreType.DMA((chips,)),
            pltpu.SemaphoreType.DMA,
        ],
        compiler_params=pltpu.CompilerParams(
            collective_id=0, has_side_effects=True, vmem_limit_bytes=56 * 2**20
        ),
        cost_estimate=pl.CostEstimate(
            flops=2 * seq_count * rows * depth * columns,
            bytes_accessed=2 * depth * columns + 2 * seq_count * rows * depth,
            transcendentals=0,
        ),
    )(*parts, out_weight)


def local(
    hidden_in,
    queries,
    image_kv,
    out_weight,
    gate,
    tile_counts,
    owners,
    starts,
    norm_gain,
    norm_grad,
    stream_grad,
):
    seq_count = lax.axis_size("seq")
    here = lax.axis_index("seq")
    tok_rows, q_width = queries.shape
    q_heads = q_width // HEAD_DIM
    kv_width = image_kv.shape[3]
    group = q_heads // (kv_width // HEAD_DIM)
    slot_count = seq_count * CAP
    owner_table = owners.reshape(seq_count, BLOCKS_DEV)
    start_table = starts.reshape(seq_count, BLOCKS_DEV)
    my_owner = lax.dynamic_index_in_dim(owner_table, here, 0, keepdims=False)
    block_ids = jnp.arange(BLOCKS_DEV)
    same = my_owner[:, None] == my_owner[None, :]
    earlier = block_ids[None, :] < block_ids[:, None]
    my_rank = jnp.sum(jnp.logical_and(same, earlier).astype(jnp.int32), axis=1)
    my_slot = my_owner * CAP + my_rank
    placing = (my_slot[:, None] == jnp.arange(slot_count)[None, :]).astype(jnp.bfloat16)
    q_blocks = queries.reshape(BLOCKS_DEV, BLK, q_width)
    outgoing = jnp.einsum(
        "bs,brc->src", placing, q_blocks, preferred_element_type=jnp.float32
    ).astype(jnp.bfloat16)
    outgoing = outgoing.reshape(seq_count, CAP, BLK, q_width)
    arriving = owner_table == here
    arrive_rank = jnp.cumsum(arriving.astype(jnp.int32), axis=1) - 1
    slot_hit = jnp.logical_and(
        arriving[:, :, None], arrive_rank[:, :, None] == jnp.arange(CAP)[None, None, :]
    )
    slot_start = jnp.sum(jnp.where(slot_hit, start_table[:, :, None], 0), axis=1)
    tile_here = lax.dynamic_index_in_dim(tile_counts, here, 0, keepdims=False)
    received = lax.all_to_all(outgoing, "seq", split_axis=0, concat_axis=0, tiled=True)
    flat = received.reshape(-1, q_width)
    slot_first = slot_start.reshape(-1)
    order = jnp.argsort(slot_first).astype(jnp.int32)
    sorted_first = slot_first[order]
    row_width = out_weight.shape[0]
    width = min(group * HEAD_DIM, row_width)
    parts = []
    for index in range(q_width // width):
        kv_head = index * width // (group * HEAD_DIM)
        mixed = attend(order, sorted_first, tile_here[None], flat, image_kv, index, width, kv_head)
        gathered = lax.all_gather(mixed, "heads", axis=0)
        parts.append(gathered.reshape(-1, seq_count, CAP * BLK, width))
    slots = project_rows(parts, out_weight, seq_count)
    branch = jnp.einsum(
        "bs,src->brc",
        placing,
        slots.reshape(slot_count, BLK, -1),
        preferred_element_type=jnp.float32,
    ).reshape(tok_rows, -1)
    hidden_out = (hidden_in.astype(jnp.float32) + jnp.tanh(gate[0]) * branch).astype(jnp.bfloat16)
    hidden = hidden_out.astype(jnp.float32)
    scaled = norm_gain[None, :] * norm_grad.astype(jnp.float32)
    squares, product = lax.psum(
        (jnp.sum(hidden * hidden, axis=1), jnp.sum(hidden * scaled, axis=1)), "heads"
    )
    inverse = lax.rsqrt(squares / D + EPS)[:, None]
    project = (product / D)[:, None]
    stream_in_grad = (
        stream_grad.astype(jnp.float32) + inverse * scaled - inverse**3 * project * hidden
    )
    return (hidden_out, stream_in_grad)


def solution(mesh):
    placed = (
        P("seq", "heads"),
        P("seq", "heads"),
        P("seq", None, None, "heads"),
        P("seq", "heads"),
        P(),
        P(),
        P(),
        P(),
        P("heads"),
        P("seq", "heads"),
        P("seq", "heads"),
    )
    return jax.shard_map(
        local,
        mesh=mesh,
        in_specs=placed,
        out_specs=(P("seq", "heads"), P("seq", "heads")),
        check_vma=False,
    )
```

```python
import functools
import math

import jax
import jax.numpy as jnp
from jax import lax
from jax.experimental import pallas as pl
from jax.experimental.pallas import tpu as pltpu
from jax.sharding import PartitionSpec as P

D = 8192
HEAD_DIM = 128
TILE_TOK = 1601
BLOCKS_DEV = 16
CAP = 2
BLK = 16


EPS = 1e-05


KEY_BLOCK = 1792
KEY_PART = 256
LANES = 128
GROUP_SLOTS = 4


def attend_body(order_ref, first_ref, tiles_ref, q_ref, k_ref, v_ref, o_ref, qs, vx, acc, top):
    step = pl.program_id(0)
    heads = q_ref.shape[1] // HEAD_DIM
    per_head = GROUP_SLOTS * BLK
    rows = heads * per_head
    factor = math.log2(math.e) / math.sqrt(HEAD_DIM)

    @pl.when(step == 0)
    def _():
        vx[:, :HEAD_DIM] = v_ref[0, 0]
        vx[:, HEAD_DIM:] = jnp.ones((vx.shape[0], HEAD_DIM), jnp.bfloat16)

    for slot in range(GROUP_SLOTS):
        place = order_ref[step * GROUP_SLOTS + slot]
        source = q_ref[pl.ds(pl.multiple_of(place * BLK, BLK), BLK), :]
        for head in range(heads):
            qs[pl.ds(head * per_head + slot * BLK, BLK), :] = source[
                :, head * HEAD_DIM : (head + 1) * HEAD_DIM
            ]
    acc[...] = jnp.zeros_like(acc)
    top[...] = jnp.full_like(top, -3e38)
    slot_of = lax.broadcasted_iota(jnp.int32, (rows, LANES), 0) % per_head // BLK
    first = jnp.zeros((rows, LANES), jnp.int32)
    lowest = first_ref[step * GROUP_SLOTS]
    for slot in range(GROUP_SLOTS):
        first = jnp.where(slot_of == slot, first_ref[step * GROUP_SLOTS + slot], first)

    @pl.loop(lowest, tiles_ref[0])
    def _(tile):
        base = pl.multiple_of(tile * TILE_TOK // LANES * LANES, LANES)
        low = tile * TILE_TOK - base
        high = low + TILE_TOK
        query = qs[...]
        parts = []
        best = None
        for part in range(KEY_BLOCK // KEY_PART):
            keys = k_ref[0, 0, pl.ds(base + part * KEY_PART, KEY_PART), :]
            scores = lax.dot_general(
                query, keys, (((1,), (1,)), ((), ())), preferred_element_type=jnp.float32
            )
            spot = lax.broadcasted_iota(jnp.int32, scores.shape, 1) + part * KEY_PART
            if part == 0:
                scores = jnp.where(spot >= low, scores, -jnp.inf)
            if (part + 1) * KEY_PART > TILE_TOK:
                scores = jnp.where(spot < high, scores, -jnp.inf)
            parts.append(scores)
            peak = jnp.maximum(scores[:, :LANES], scores[:, LANES:])
            best = peak if best is None else jnp.maximum(best, peak)
        before = top[...]
        seen = first <= tile
        highest = jnp.maximum(before, jnp.max(best, axis=1, keepdims=True))
        highest = jnp.where(seen, highest, before)
        top[...] = highest
        alpha = jnp.exp2((before - highest) * factor)
        shift = jnp.where(seen, highest * factor, jnp.inf)
        shift = jnp.concatenate([shift, shift], axis=1)
        mixed = None
        for part in range(KEY_BLOCK // KEY_PART):
            probs = jnp.exp2(parts[part] * factor - shift).astype(jnp.bfloat16)
            values = vx[pl.ds(base + part * KEY_PART, KEY_PART), :]
            term = jnp.dot(probs, values, preferred_element_type=jnp.float32)
            mixed = term if mixed is None else mixed + term
        acc[...] = acc[...] * jnp.concatenate([alpha, alpha], axis=1) + mixed

    result = (acc[:, :HEAD_DIM] / acc[:, HEAD_DIM:]).astype(jnp.bfloat16)
    for slot in range(GROUP_SLOTS):
        place = order_ref[step * GROUP_SLOTS + slot]
        for head in range(heads):
            start = head * per_head + slot * BLK
            o_ref[
                pl.ds(pl.multiple_of(place * BLK, BLK), BLK),
                head * HEAD_DIM : (head + 1) * HEAD_DIM,
            ] = result[start : start + BLK]


def attend(order, first, tiles, flat, image_kv, index, width, kv_head):
    rows = flat.shape[0]
    keys = image_kv.shape[2]
    stacked = width // HEAD_DIM * GROUP_SLOTS * BLK
    return pl.pallas_call(
        attend_body,
        grid_spec=pltpu.PrefetchScalarGridSpec(
            num_scalar_prefetch=3,
            grid=(rows // (GROUP_SLOTS * BLK),),
            in_specs=[
                pl.BlockSpec((rows, width), lambda g, *_: (0, index)),
                pl.BlockSpec((1, 1, keys, HEAD_DIM), lambda g, *_: (0, 0, 0, kv_head)),
                pl.BlockSpec((1, 1, keys, HEAD_DIM), lambda g, *_: (0, 1, 0, kv_head)),
            ],
            out_specs=pl.BlockSpec((rows, width), lambda g, *_: (0, 0)),
            scratch_shapes=[
                pltpu.VMEM((stacked, HEAD_DIM), jnp.bfloat16),
                pltpu.VMEM((keys, 2 * HEAD_DIM), jnp.bfloat16),
                pltpu.VMEM((stacked, 2 * HEAD_DIM), jnp.float32),
                pltpu.VMEM((stacked, LANES), jnp.float32),
            ],
        ),
        out_shape=jax.ShapeDtypeStruct((rows, width), jnp.bfloat16),
        compiler_params=pltpu.CompilerParams(vmem_limit_bytes=60 * 2**20),
        cost_estimate=pl.CostEstimate(
            flops=4 * rows * width * keys,
            bytes_accessed=4 * keys * HEAD_DIM + 4 * rows * width,
            transcendentals=rows * width // HEAD_DIM * keys,
        ),
    )(order, first, tiles, flat, image_kv, image_kv)


def project_body(seq_count, count, *refs):
    parts = refs[:count]
    w_ref, o_ref = refs[count : count + 2]
    (held, stage, paired, summed, landed, own, gathered) = refs[count + 2 : count + 9]
    (send_a, recv_a, send_p, recv_p, send_s, recv_s, local_sem, send_z, recv_z) = refs[count + 9 :]
    plane, planes = lax.axis_index("heads"), gathered.shape[1]
    me = lax.axis_index("seq")
    chips = seq_count // 2
    chip, core = me // 2, lax.rem(me, 2)
    sibling = chip * 2 + 1 - core
    splits = count
    rows, columns = own.shape
    tile = 512
    barrier = pltpu.get_barrier_semaphore()
    for step in range(1, seq_count):
        pl.semaphore_signal(
            barrier,
            inc=1,
            device_id={"seq": lax.rem(me + step, seq_count)},
            device_id_type=pl.DeviceIdType.MESH,
        )
    ways = (1, -1)

    def inside(index):
        return jnp.logical_and(index >= 0, index < planes)

    for way in ways:
        @pl.when(inside(plane + way))
        def _():
            pl.semaphore_signal(
                barrier,
                inc=1,
                device_id={"heads": plane + way},
                device_id_type=pl.DeviceIdType.MESH,
            )

    others = sum(inside(plane + way).astype(jnp.int32) for way in ways)
    pl.semaphore_wait(barrier, seq_count - 1 + others)

    def plane_copy(source, way, part, hop):
        origin = plane - way * (hop - 1)
        return pltpu.make_async_remote_copy(
            src_ref=source,
            dst_ref=gathered.at[part, origin],
            send_sem=send_z.at[max(way, 0), part, hop],
            recv_sem=recv_z.at[max(way, 0), part, hop],
            device_id={"heads": plane + way},
            device_id_type=pl.DeviceIdType.MESH,
        )

    def context_copy(source, target):
        return pltpu.make_async_remote_copy(
            src_ref=source,
            dst_ref=held.at[:, me],
            send_sem=send_a.at[target],
            recv_sem=recv_a.at[me],
            device_id={"seq": target},
            device_id_type=pl.DeviceIdType.MESH,
        )

    def deliver(source, target):
        @pl.when(target != me)
        def _():
            context_copy(source, target).start()

        @pl.when(target == me)
        def _():
            kept = pltpu.make_async_copy(source, held.at[:, me], local_sem)
            kept.start()
            kept.wait()

    for part in range(splits):
        for way in ways:
            @pl.when(inside(plane + way))
            def _():
                plane_copy(parts[part], way, part, 1).start()

    for part in range(splits):
        deliver(parts[part], plane * splits + part)

    for hop in range(1, planes):
        for part in range(splits):
            for way in ways:
                origin = plane - way * hop

                @pl.when(inside(origin))
                def _():
                    block = gathered.at[part, origin]
                    pltpu.make_async_remote_copy(
                        src_ref=block,
                        dst_ref=block,
                        send_sem=send_z.at[max(way, 0), part, hop],
                        recv_sem=recv_z.at[max(way, 0), part, hop],
                        device_id={"heads": plane - way},
                        device_id_type=pl.DeviceIdType.MESH,
                    ).wait_recv()

                    if hop + 1 < planes:
                        @pl.when(inside(plane + way))
                        def _():
                            plane_copy(block, way, part, hop + 1).start()

                    deliver(block, origin * splits + part)

    for step in range(1, seq_count):
        source = lax.rem(me + seq_count - step, seq_count)
        pltpu.make_async_remote_copy(
            src_ref=parts[0],
            dst_ref=held.at[:, source],
            send_sem=send_a.at[source],
            recv_sem=recv_a.at[source],
            device_id={"seq": source},
            device_id_type=pl.DeviceIdType.MESH,
        ).wait_recv()

    def product(target, start):
        left = held[target].reshape(rows, held.shape[3])
        return jnp.dot(
            left, w_ref[:, pl.ds(start, tile)], preferred_element_type=jnp.float32
        )

    def target_chip(step):
        return lax.rem(chip + 1 + step, chips)

    def pair_copy(step):
        return pltpu.make_async_remote_copy(
            src_ref=stage.at[step],
            dst_ref=paired.at[step],
            send_sem=send_p.at[step],
            recv_sem=recv_p.at[step],
            device_id={"seq": sibling},
            device_id_type=pl.DeviceIdType.MESH,
        )

    def sum_copy(step):
        return pltpu.make_async_remote_copy(
            src_ref=summed.at[step],
            dst_ref=landed.at[step],
            send_sem=send_s.at[step],
            recv_sem=recv_s.at[step],
            device_id={"seq": target_chip(step) * 2 + core},
            device_id_type=pl.DeviceIdType.MESH,
        )

    def give(step):
        @pl.loop(0, columns // tile)
        def _(index):
            start = pl.multiple_of(index * tile, tile)
            stage[step, :, pl.ds(start, tile)] = product(
                target_chip(step) * 2 + 1 - core, start
            ).astype(jnp.bfloat16)

        pair_copy(step).start()

    give(0)
    for step in range(chips):
        if step + 1 < chips:
            give(step + 1)

        @pl.loop(0, columns // tile)
        def _(index):
            start = pl.multiple_of(index * tile, tile)
            own[:, pl.ds(start, tile)] = product(target_chip(step) * 2 + core, start)

        pair_copy(step).wait_recv()
        if step + 1 < chips:
            @pl.loop(0, columns // tile)
            def _(index):
                span = pl.ds(pl.multiple_of(index * tile, tile), tile)
                total = own[:, span] + paired[step, :, span].astype(jnp.float32)
                summed[step, :, span] = total.astype(jnp.bfloat16)

            sum_copy(step).start()

    for step in range(chips - 1):
        sum_copy(step).wait_recv()

    @pl.loop(0, columns // tile)
    def _(index):
        span = pl.ds(pl.multiple_of(index * tile, tile), tile)
        total = own[:, span] + paired[chips - 1, :, span].astype(jnp.float32)
        for step in range(chips - 1):
            total = total + landed[step, :, span].astype(jnp.float32)
        o_ref[:, span] = total.astype(jnp.bfloat16)

    for step in range(1, seq_count):
        context_copy(parts[0], lax.rem(me + step, seq_count)).wait_send()
    for hop in range(1, planes):
        for part in range(splits):
            for way in ways:
                sent = jnp.logical_and(inside(plane - way * (hop - 1)), inside(plane + way))

                @pl.when(sent)
                def _():
                    plane_copy(parts[part], way, part, hop).wait_send()
    for step in range(chips):
        pair_copy(step).wait_send()
    for step in range(chips - 1):
        sum_copy(step).wait_send()


def project_rows(parts, out_weight, seq_count):
    count = len(parts)
    depth, columns = out_weight.shape
    piece = parts[0].shape[1]
    planes = lax.axis_size("heads")
    rows = seq_count * piece
    chips = seq_count // 2
    return pl.pallas_call(
        functools.partial(project_body, seq_count, count),
        in_specs=[pl.BlockSpec(memory_space=pl.ANY)] * count
        + [pl.BlockSpec(memory_space=pltpu.VMEM)],
        out_specs=pl.BlockSpec(memory_space=pltpu.VMEM),
        out_shape=jax.ShapeDtypeStruct((rows, columns), jnp.bfloat16),
        scratch_shapes=[
            pltpu.VMEM((seq_count, seq_count, piece, depth), jnp.bfloat16),
            pltpu.VMEM((chips, rows, columns), jnp.bfloat16),
            pltpu.VMEM((chips, rows, columns), jnp.bfloat16),
            pltpu.VMEM((chips - 1, rows, columns), jnp.bfloat16),
            pltpu.VMEM((chips - 1, rows, columns), jnp.bfloat16),
            pltpu.VMEM((rows, columns), jnp.float32),
            pltpu.VMEM((count, planes, seq_count, piece, depth), jnp.bfloat16),
            pltpu.SemaphoreType.DMA((seq_count,)),
            pltpu.SemaphoreType.DMA((seq_count,)),
            pltpu.SemaphoreType.DMA((chips,)),
            pltpu.SemaphoreType.DMA((chips,)),
            pltpu.SemaphoreType.DMA((chips,)),
            pltpu.SemaphoreType.DMA((chips,)),
            pltpu.SemaphoreType.DMA,
            pltpu.SemaphoreType.DMA((2, count, planes)),
            pltpu.SemaphoreType.DMA((2, count, planes)),
        ],
        compiler_params=pltpu.CompilerParams(
            collective_id=0, has_side_effects=True, vmem_limit_bytes=56 * 2**20
        ),
        cost_estimate=pl.CostEstimate(
            flops=2 * seq_count * rows * depth * columns,
            bytes_accessed=2 * depth * columns + 2 * seq_count * rows * depth,
            transcendentals=0,
        ),
    )(*parts, out_weight)


def local(
    hidden_in,
    queries,
    image_kv,
    out_weight,
    gate,
    tile_counts,
    owners,
    starts,
    norm_gain,
    norm_grad,
    stream_grad,
):
    seq_count = lax.axis_size("seq")
    here = lax.axis_index("seq")
    tok_rows, q_width = queries.shape
    q_heads = q_width // HEAD_DIM
    kv_width = image_kv.shape[3]
    group = q_heads // (kv_width // HEAD_DIM)
    slot_count = seq_count * CAP
    owner_table = owners.reshape(seq_count, BLOCKS_DEV)
    start_table = starts.reshape(seq_count, BLOCKS_DEV)
    my_owner = lax.dynamic_index_in_dim(owner_table, here, 0, keepdims=False)
    block_ids = jnp.arange(BLOCKS_DEV)
    same = my_owner[:, None] == my_owner[None, :]
    earlier = block_ids[None, :] < block_ids[:, None]
    my_rank = jnp.sum(jnp.logical_and(same, earlier).astype(jnp.int32), axis=1)
    my_slot = my_owner * CAP + my_rank
    placing = (my_slot[:, None] == jnp.arange(slot_count)[None, :]).astype(jnp.bfloat16)
    q_blocks = queries.reshape(BLOCKS_DEV, BLK, q_width)
    outgoing = jnp.einsum(
        "bs,brc->src", placing, q_blocks, preferred_element_type=jnp.float32
    ).astype(jnp.bfloat16)
    outgoing = outgoing.reshape(seq_count, CAP, BLK, q_width)
    arriving = owner_table == here
    arrive_rank = jnp.cumsum(arriving.astype(jnp.int32), axis=1) - 1
    slot_hit = jnp.logical_and(
        arriving[:, :, None], arrive_rank[:, :, None] == jnp.arange(CAP)[None, None, :]
    )
    slot_start = jnp.sum(jnp.where(slot_hit, start_table[:, :, None], 0), axis=1)
    tile_here = lax.dynamic_index_in_dim(tile_counts, here, 0, keepdims=False)
    received = lax.all_to_all(outgoing, "seq", split_axis=0, concat_axis=0, tiled=True)
    flat = received.reshape(-1, q_width)
    slot_first = slot_start.reshape(-1)
    order = jnp.argsort(slot_first).astype(jnp.int32)
    sorted_first = slot_first[order]
    row_width = out_weight.shape[0]
    width = min(group * HEAD_DIM, row_width)
    parts = []
    for index in range(q_width // width):
        kv_head = index * width // (group * HEAD_DIM)
        mixed = attend(order, sorted_first, tile_here[None], flat, image_kv, index, width, kv_head)
        parts.append(mixed.reshape(seq_count, CAP * BLK, width))
    slots = project_rows(parts, out_weight, seq_count)
    branch = jnp.einsum(
        "bs,src->brc",
        placing,
        slots.reshape(slot_count, BLK, -1),
        preferred_element_type=jnp.float32,
    ).reshape(tok_rows, -1)
    hidden_out = (hidden_in.astype(jnp.float32) + jnp.tanh(gate[0]) * branch).astype(jnp.bfloat16)
    hidden = hidden_out.astype(jnp.float32)
    scaled = norm_gain[None, :] * norm_grad.astype(jnp.float32)
    squares, product = lax.psum(
        (jnp.sum(hidden * hidden, axis=1), jnp.sum(hidden * scaled, axis=1)), "heads"
    )
    inverse = lax.rsqrt(squares / D + EPS)[:, None]
    project = (product / D)[:, None]
    stream_in_grad = (
        stream_grad.astype(jnp.float32) + inverse * scaled - inverse**3 * project * hidden
    )
    return (hidden_out, stream_in_grad)


def solution(mesh):
    placed = (
        P("seq", "heads"),
        P("seq", "heads"),
        P("seq", None, None, "heads"),
        P("seq", "heads"),
        P(),
        P(),
        P(),
        P(),
        P("heads"),
        P("seq", "heads"),
        P("seq", "heads"),
    )
    return jax.shard_map(
        local,
        mesh=mesh,
        in_specs=placed,
        out_specs=(P("seq", "heads"), P("seq", "heads")),
        check_vma=False,
    )
```

```python
import functools
import math

import jax
import jax.numpy as jnp
from jax import lax
from jax.experimental import pallas as pl
from jax.experimental.pallas import tpu as pltpu
from jax.sharding import PartitionSpec as P

D = 8192
HEAD_DIM = 128
TILE_TOK = 1601
BLOCKS_DEV = 16
CAP = 2
BLK = 16


EPS = 1e-05


KEY_BLOCK = 1792
KEY_PART = 256
LANES = 128
GROUP_SLOTS = 4


def attend_body(order_ref, first_ref, tiles_ref, q_ref, k_ref, v_ref, o_ref, qs, vx, acc, top):
    step = pl.program_id(0)
    heads = q_ref.shape[1] // HEAD_DIM
    per_head = GROUP_SLOTS * BLK
    rows = heads * per_head
    factor = math.log2(math.e) / math.sqrt(HEAD_DIM)

    @pl.when(step == 0)
    def _():
        vx[:, :HEAD_DIM] = v_ref[0, 0]
        vx[:, HEAD_DIM:] = jnp.ones((vx.shape[0], HEAD_DIM), jnp.bfloat16)

    for slot in range(GROUP_SLOTS):
        place = order_ref[step * GROUP_SLOTS + slot]
        source = q_ref[pl.ds(pl.multiple_of(place * BLK, BLK), BLK), :]
        for head in range(heads):
            qs[pl.ds(head * per_head + slot * BLK, BLK), :] = source[
                :, head * HEAD_DIM : (head + 1) * HEAD_DIM
            ]
    acc[...] = jnp.zeros_like(acc)
    top[...] = jnp.full_like(top, -3e38)
    slot_of = lax.broadcasted_iota(jnp.int32, (rows, LANES), 0) % per_head // BLK
    first = jnp.zeros((rows, LANES), jnp.int32)
    lowest = first_ref[step * GROUP_SLOTS]
    for slot in range(GROUP_SLOTS):
        first = jnp.where(slot_of == slot, first_ref[step * GROUP_SLOTS + slot], first)

    @pl.loop(lowest, tiles_ref[0])
    def _(tile):
        base = pl.multiple_of(tile * TILE_TOK // LANES * LANES, LANES)
        low = tile * TILE_TOK - base
        high = low + TILE_TOK
        query = qs[...]
        parts = []
        best = None
        for part in range(KEY_BLOCK // KEY_PART):
            keys = k_ref[0, 0, pl.ds(base + part * KEY_PART, KEY_PART), :]
            scores = lax.dot_general(
                query, keys, (((1,), (1,)), ((), ())), preferred_element_type=jnp.float32
            )
            spot = lax.broadcasted_iota(jnp.int32, scores.shape, 1) + part * KEY_PART
            if part == 0:
                scores = jnp.where(spot >= low, scores, -jnp.inf)
            if (part + 1) * KEY_PART > TILE_TOK:
                scores = jnp.where(spot < high, scores, -jnp.inf)
            parts.append(scores)
            peak = jnp.maximum(scores[:, :LANES], scores[:, LANES:])
            best = peak if best is None else jnp.maximum(best, peak)
        before = top[...]
        seen = first <= tile
        highest = jnp.maximum(before, jnp.max(best, axis=1, keepdims=True))
        highest = jnp.where(seen, highest, before)
        top[...] = highest
        alpha = jnp.exp2((before - highest) * factor)
        shift = jnp.where(seen, highest * factor, jnp.inf)
        shift = jnp.concatenate([shift, shift], axis=1)
        mixed = None
        for part in range(KEY_BLOCK // KEY_PART):
            probs = jnp.exp2(parts[part] * factor - shift).astype(jnp.bfloat16)
            values = vx[pl.ds(base + part * KEY_PART, KEY_PART), :]
            term = jnp.dot(probs, values, preferred_element_type=jnp.float32)
            mixed = term if mixed is None else mixed + term
        acc[...] = acc[...] * jnp.concatenate([alpha, alpha], axis=1) + mixed

    result = (acc[:, :HEAD_DIM] / acc[:, HEAD_DIM:]).astype(jnp.bfloat16)
    for slot in range(GROUP_SLOTS):
        place = order_ref[step * GROUP_SLOTS + slot]
        for head in range(heads):
            start = head * per_head + slot * BLK
            o_ref[
                pl.ds(pl.multiple_of(place * BLK, BLK), BLK),
                head * HEAD_DIM : (head + 1) * HEAD_DIM,
            ] = result[start : start + BLK]


def attend(order, first, tiles, flat, image_kv, index, width, kv_head):
    rows = flat.shape[0]
    keys = image_kv.shape[2]
    stacked = width // HEAD_DIM * GROUP_SLOTS * BLK
    return pl.pallas_call(
        attend_body,
        grid_spec=pltpu.PrefetchScalarGridSpec(
            num_scalar_prefetch=3,
            grid=(rows // (GROUP_SLOTS * BLK),),
            in_specs=[
                pl.BlockSpec((rows, width), lambda g, *_: (0, index)),
                pl.BlockSpec((1, 1, keys, HEAD_DIM), lambda g, *_: (0, 0, 0, kv_head)),
                pl.BlockSpec((1, 1, keys, HEAD_DIM), lambda g, *_: (0, 1, 0, kv_head)),
            ],
            out_specs=pl.BlockSpec((rows, width), lambda g, *_: (0, 0)),
            scratch_shapes=[
                pltpu.VMEM((stacked, HEAD_DIM), jnp.bfloat16),
                pltpu.VMEM((keys, 2 * HEAD_DIM), jnp.bfloat16),
                pltpu.VMEM((stacked, 2 * HEAD_DIM), jnp.float32),
                pltpu.VMEM((stacked, LANES), jnp.float32),
            ],
        ),
        out_shape=jax.ShapeDtypeStruct((rows, width), jnp.bfloat16),
        compiler_params=pltpu.CompilerParams(vmem_limit_bytes=60 * 2**20),
        cost_estimate=pl.CostEstimate(
            flops=4 * rows * width * keys,
            bytes_accessed=4 * keys * HEAD_DIM + 4 * rows * width,
            transcendentals=rows * width // HEAD_DIM * keys,
        ),
    )(order, first, tiles, flat, image_kv, image_kv)


def project_body(seq_count, count, *refs):
    parts = refs[:count]
    w_ref, o_ref = refs[count : count + 2]
    (held, stage, paired, summed, landed, own, gathered) = refs[count + 2 : count + 9]
    (send_a, recv_a, send_p, recv_p, send_s, recv_s, local_sem, send_z, recv_z) = refs[count + 9 :]
    plane, planes = lax.axis_index("heads"), gathered.shape[1]
    me = lax.axis_index("seq")
    chips = seq_count // 2
    chip, core = me // 2, lax.rem(me, 2)
    sibling = chip * 2 + 1 - core
    splits = count
    rows, columns = own.shape
    tile = 512
    barrier = pltpu.get_barrier_semaphore()
    for step in range(1, seq_count):
        pl.semaphore_signal(
            barrier,
            inc=1,
            device_id={"seq": lax.rem(me + step, seq_count)},
            device_id_type=pl.DeviceIdType.MESH,
        )
    ways = (1, -1)

    def inside(index):
        return jnp.logical_and(index >= 0, index < planes)

    for way in ways:
        @pl.when(inside(plane + way))
        def _():
            pl.semaphore_signal(
                barrier,
                inc=1,
                device_id={"heads": plane + way},
                device_id_type=pl.DeviceIdType.MESH,
            )

    others = sum(inside(plane + way).astype(jnp.int32) for way in ways)
    pl.semaphore_wait(barrier, seq_count - 1 + others)

    def plane_copy(source, way, part, hop):
        origin = plane - way * (hop - 1)
        return pltpu.make_async_remote_copy(
            src_ref=source,
            dst_ref=gathered.at[part, origin],
            send_sem=send_z.at[max(way, 0), part, hop],
            recv_sem=recv_z.at[max(way, 0), part, hop],
            device_id={"heads": plane + way},
            device_id_type=pl.DeviceIdType.MESH,
        )

    def context_copy(source, target):
        return pltpu.make_async_remote_copy(
            src_ref=source,
            dst_ref=held.at[:, me],
            send_sem=send_a.at[target],
            recv_sem=recv_a.at[me],
            device_id={"seq": target},
            device_id_type=pl.DeviceIdType.MESH,
        )

    def deliver(source, target):
        @pl.when(target != me)
        def _():
            context_copy(source, target).start()

        @pl.when(target == me)
        def _():
            kept = pltpu.make_async_copy(source, held.at[:, me], local_sem)
            kept.start()
            kept.wait()

    for part in range(1, splits):
        for way in ways:
            @pl.when(inside(plane + way))
            def _():
                plane_copy(parts[part], way, part, 1).start()

    for shift in range(planes):
        first = lax.rem(plane + shift, planes)
        deliver(parts[0].at[first], first * splits)
    for part in range(1, splits):
        deliver(parts[part], plane * splits + part)

    for hop in range(1, planes):
        for part in range(1, splits):
            for way in ways:
                origin = plane - way * hop

                @pl.when(inside(origin))
                def _():
                    block = gathered.at[part, origin]
                    pltpu.make_async_remote_copy(
                        src_ref=block,
                        dst_ref=block,
                        send_sem=send_z.at[max(way, 0), part, hop],
                        recv_sem=recv_z.at[max(way, 0), part, hop],
                        device_id={"heads": plane - way},
                        device_id_type=pl.DeviceIdType.MESH,
                    ).wait_recv()

                    if hop + 1 < planes:
                        @pl.when(inside(plane + way))
                        def _():
                            plane_copy(block, way, part, hop + 1).start()

                    deliver(block, origin * splits + part)

    for step in range(1, seq_count):
        source = lax.rem(me + seq_count - step, seq_count)
        pltpu.make_async_remote_copy(
            src_ref=parts[-1],
            dst_ref=held.at[:, source],
            send_sem=send_a.at[source],
            recv_sem=recv_a.at[source],
            device_id={"seq": source},
            device_id_type=pl.DeviceIdType.MESH,
        ).wait_recv()

    def product(target, start):
        left = held[target].reshape(rows, held.shape[3])
        return jnp.dot(
            left, w_ref[:, pl.ds(start, tile)], preferred_element_type=jnp.float32
        )

    def target_chip(step):
        return lax.rem(chip + 1 + step, chips)

    def pair_copy(step):
        return pltpu.make_async_remote_copy(
            src_ref=stage.at[step],
            dst_ref=paired.at[step],
            send_sem=send_p.at[step],
            recv_sem=recv_p.at[step],
            device_id={"seq": sibling},
            device_id_type=pl.DeviceIdType.MESH,
        )

    def sum_copy(step):
        return pltpu.make_async_remote_copy(
            src_ref=summed.at[step],
            dst_ref=landed.at[step],
            send_sem=send_s.at[step],
            recv_sem=recv_s.at[step],
            device_id={"seq": target_chip(step) * 2 + core},
            device_id_type=pl.DeviceIdType.MESH,
        )

    def give(step):
        @pl.loop(0, columns // tile)
        def _(index):
            start = pl.multiple_of(index * tile, tile)
            stage[step, :, pl.ds(start, tile)] = product(
                target_chip(step) * 2 + 1 - core, start
            ).astype(jnp.bfloat16)

        pair_copy(step).start()

    give(0)
    for step in range(chips):
        if step + 1 < chips:
            give(step + 1)

        @pl.loop(0, columns // tile)
        def _(index):
            start = pl.multiple_of(index * tile, tile)
            own[:, pl.ds(start, tile)] = product(target_chip(step) * 2 + core, start)

        pair_copy(step).wait_recv()
        if step + 1 < chips:
            @pl.loop(0, columns // tile)
            def _(index):
                span = pl.ds(pl.multiple_of(index * tile, tile), tile)
                total = own[:, span] + paired[step, :, span].astype(jnp.float32)
                summed[step, :, span] = total.astype(jnp.bfloat16)

            sum_copy(step).start()

    for step in range(chips - 1):
        sum_copy(step).wait_recv()

    @pl.loop(0, columns // tile)
    def _(index):
        span = pl.ds(pl.multiple_of(index * tile, tile), tile)
        total = own[:, span] + paired[chips - 1, :, span].astype(jnp.float32)
        for step in range(chips - 1):
            total = total + landed[step, :, span].astype(jnp.float32)
        o_ref[:, span] = total.astype(jnp.bfloat16)

    for step in range(1, seq_count):
        context_copy(parts[-1], lax.rem(me + step, seq_count)).wait_send()
    for hop in range(1, planes):
        for part in range(1, splits):
            for way in ways:
                sent = jnp.logical_and(inside(plane - way * (hop - 1)), inside(plane + way))

                @pl.when(sent)
                def _():
                    plane_copy(parts[part], way, part, hop).wait_send()
    for step in range(chips):
        pair_copy(step).wait_send()
    for step in range(chips - 1):
        sum_copy(step).wait_send()


def project_rows(parts, out_weight, seq_count):
    count = len(parts)
    depth, columns = out_weight.shape
    piece = parts[-1].shape[1]
    planes = lax.axis_size("heads")
    rows = seq_count * piece
    chips = seq_count // 2
    return pl.pallas_call(
        functools.partial(project_body, seq_count, count),
        in_specs=[pl.BlockSpec(memory_space=pl.ANY)] * count
        + [pl.BlockSpec(memory_space=pltpu.VMEM)],
        out_specs=pl.BlockSpec(memory_space=pltpu.VMEM),
        out_shape=jax.ShapeDtypeStruct((rows, columns), jnp.bfloat16),
        scratch_shapes=[
            pltpu.VMEM((seq_count, seq_count, piece, depth), jnp.bfloat16),
            pltpu.VMEM((chips, rows, columns), jnp.bfloat16),
            pltpu.VMEM((chips, rows, columns), jnp.bfloat16),
            pltpu.VMEM((chips - 1, rows, columns), jnp.bfloat16),
            pltpu.VMEM((chips - 1, rows, columns), jnp.bfloat16),
            pltpu.VMEM((rows, columns), jnp.float32),
            pltpu.VMEM((count, planes, seq_count, piece, depth), jnp.bfloat16),
            pltpu.SemaphoreType.DMA((seq_count,)),
            pltpu.SemaphoreType.DMA((seq_count,)),
            pltpu.SemaphoreType.DMA((chips,)),
            pltpu.SemaphoreType.DMA((chips,)),
            pltpu.SemaphoreType.DMA((chips,)),
            pltpu.SemaphoreType.DMA((chips,)),
            pltpu.SemaphoreType.DMA,
            pltpu.SemaphoreType.DMA((2, count, planes)),
            pltpu.SemaphoreType.DMA((2, count, planes)),
        ],
        compiler_params=pltpu.CompilerParams(
            collective_id=0, has_side_effects=True, vmem_limit_bytes=56 * 2**20
        ),
        cost_estimate=pl.CostEstimate(
            flops=2 * seq_count * rows * depth * columns,
            bytes_accessed=2 * depth * columns + 2 * seq_count * rows * depth,
            transcendentals=0,
        ),
    )(*parts, out_weight)


def local(
    hidden_in,
    queries,
    image_kv,
    out_weight,
    gate,
    tile_counts,
    owners,
    starts,
    norm_gain,
    norm_grad,
    stream_grad,
):
    seq_count = lax.axis_size("seq")
    here = lax.axis_index("seq")
    tok_rows, q_width = queries.shape
    q_heads = q_width // HEAD_DIM
    kv_width = image_kv.shape[3]
    group = q_heads // (kv_width // HEAD_DIM)
    slot_count = seq_count * CAP
    owner_table = owners.reshape(seq_count, BLOCKS_DEV)
    start_table = starts.reshape(seq_count, BLOCKS_DEV)
    my_owner = lax.dynamic_index_in_dim(owner_table, here, 0, keepdims=False)
    block_ids = jnp.arange(BLOCKS_DEV)
    same = my_owner[:, None] == my_owner[None, :]
    earlier = block_ids[None, :] < block_ids[:, None]
    my_rank = jnp.sum(jnp.logical_and(same, earlier).astype(jnp.int32), axis=1)
    my_slot = my_owner * CAP + my_rank
    placing = (my_slot[:, None] == jnp.arange(slot_count)[None, :]).astype(jnp.bfloat16)
    q_blocks = queries.reshape(BLOCKS_DEV, BLK, q_width)
    outgoing = jnp.einsum(
        "bs,brc->src", placing, q_blocks, preferred_element_type=jnp.float32
    ).astype(jnp.bfloat16)
    outgoing = outgoing.reshape(seq_count, CAP, BLK, q_width)
    arriving = owner_table == here
    arrive_rank = jnp.cumsum(arriving.astype(jnp.int32), axis=1) - 1
    slot_hit = jnp.logical_and(
        arriving[:, :, None], arrive_rank[:, :, None] == jnp.arange(CAP)[None, None, :]
    )
    slot_start = jnp.sum(jnp.where(slot_hit, start_table[:, :, None], 0), axis=1)
    tile_here = lax.dynamic_index_in_dim(tile_counts, here, 0, keepdims=False)
    received = lax.all_to_all(outgoing, "seq", split_axis=0, concat_axis=0, tiled=True)
    flat = received.reshape(-1, q_width)
    slot_first = slot_start.reshape(-1)
    order = jnp.argsort(slot_first).astype(jnp.int32)
    sorted_first = slot_first[order]
    row_width = out_weight.shape[0]
    width = min(group * HEAD_DIM, row_width)
    parts = []
    for index in range(q_width // width):
        kv_head = index * width // (group * HEAD_DIM)
        mixed = attend(order, sorted_first, tile_here[None], flat, image_kv, index, width, kv_head)
        if index == 0:
            mixed = lax.all_gather(mixed, "heads", axis=0)
            parts.append(mixed.reshape(-1, seq_count, CAP * BLK, width))
        else:
            parts.append(mixed.reshape(seq_count, CAP * BLK, width))
    slots = project_rows(parts, out_weight, seq_count)
    branch = jnp.einsum(
        "bs,src->brc",
        placing,
        slots.reshape(slot_count, BLK, -1),
        preferred_element_type=jnp.float32,
    ).reshape(tok_rows, -1)
    hidden_out = (hidden_in.astype(jnp.float32) + jnp.tanh(gate[0]) * branch).astype(jnp.bfloat16)
    hidden = hidden_out.astype(jnp.float32)
    scaled = norm_gain[None, :] * norm_grad.astype(jnp.float32)
    squares, product = lax.psum(
        (jnp.sum(hidden * hidden, axis=1), jnp.sum(hidden * scaled, axis=1)), "heads"
    )
    inverse = lax.rsqrt(squares / D + EPS)[:, None]
    project = (product / D)[:, None]
    stream_in_grad = (
        stream_grad.astype(jnp.float32) + inverse * scaled - inverse**3 * project * hidden
    )
    return (hidden_out, stream_in_grad)


def solution(mesh):
    placed = (
        P("seq", "heads"),
        P("seq", "heads"),
        P("seq", None, None, "heads"),
        P("seq", "heads"),
        P(),
        P(),
        P(),
        P(),
        P("heads"),
        P("seq", "heads"),
        P("seq", "heads"),
    )
    return jax.shard_map(
        local,
        mesh=mesh,
        in_specs=placed,
        out_specs=(P("seq", "heads"), P("seq", "heads")),
        check_vma=False,
    )
```
